1024 devices in a mesh: group: 16 (over y, x_lo, core), local: 64 (over z, x_hi).
Axes of the slice: x: 4 (x_hi: 2, x_lo: 2; x = x_hi * 2 + x_lo), y: 4, z: 32, core: 2. Of those that a mesh axis runs over, the one named last changes fastest.
Arguments:
- grad_out: bfloat16 [2048, 3584], P(('group', 'local')), may hold values from -6 to 6
- routes: int32 [2048, 8], replicated, may hold values from 0 to 127, as said below
- router_weights: float32 [2048, 8], replicated, may hold values from 0.05 to 0.5
- gate_weight: bfloat16 [1024, 3584, 128], P(('group', 'local')), may hold values from -0.09375 to 0.09375
- up_weight: bfloat16 [1024, 3584, 128], P(('group', 'local')), may hold values from -0.09375 to 0.09375
- down_weight: bfloat16 [1024, 128, 3584], P(('group', 'local')), may hold values from -0.1875 to 0.1875
- saved_gate: bfloat16 [1024, 256, 128], P(('group', 'local')), may hold values from -6 to 6
- saved_up: bfloat16 [1024, 256, 128], P(('group', 'local')), may hold values from -6 to 6
Outputs:
- grad_in: bfloat16 [2048, 3584], P(('group', 'local'))
- grad_gate: bfloat16 [2048, 8], P(('group', 'local'))
The draws below stay inside these ranges and needn't reach their ends.
Inputs may be any that keep to these rules, and one draw needn't show every extreme that they name: `routes`: each token names 8 different experts, two in each of 4 different groups. Of the tokens that share one local index, every group is named by exactly 8, and at most 4 name one expert; in every group two experts are named by exactly 4 of them for every local index.
All inputs are finite; a program needn't handle non-finite values.
Results may differ from the reference program's by a relative error of at most 0.0075.
Values may be sent and summed in bfloat16 or wider, within the bound.
A program may use at most 32 MiB of HBM per device.

```python
import jax
import jax.numpy as jnp
from jax import lax

D = 3584
HID_DEV = 128
EXP_GROUP = 8
TOPG = 4
TOK_DEV = 2
TOPK = 8
HSPLIT = 8
HID = 1024
CAP = 4
SLOTS = 256
TOKENS = 2048
N_GROUP = 16
N_LOCAL = 64
DEVICES = 1024


def draw_routes(key, part):
    key = jax.random.fold_in(key, 7)
    key_column, key_indicator, key_lower = jax.random.split(key, 3)
    column_perm = jax.vmap(lambda subkey: jax.random.permutation(subkey, N_GROUP))(jax.random.split(key_column, N_LOCAL))
    hot_order = jax.vmap(lambda subkey: jax.random.permutation(subkey, EXP_GROUP))(jax.random.split(key_indicator, N_GROUP))
    lower_pick = jax.vmap(lambda subkey: jax.random.permutation(subkey, 2 * (EXP_GROUP - 2)))(jax.random.split(key_lower, N_GROUP * N_LOCAL)).reshape(N_GROUP, N_LOCAL, 2 * (EXP_GROUP - 2))
    source = jnp.arange(N_GROUP, dtype=jnp.int32)[:, None, None, None]
    column = jnp.arange(N_LOCAL, dtype=jnp.int32)[None, :, None, None]
    within = jnp.arange(TOK_DEV, dtype=jnp.int32)[None, None, :, None]
    choice_ids = jnp.arange(TOPG, dtype=jnp.int32)[None, None, None, :]
    order_index = within * TOPG + choice_ids
    chosen = column_perm[column, (source + order_index) % N_GROUP]
    half_count = TOPG * TOK_DEV // 2
    first_rank = order_index // half_count
    second_rank = 2 + lower_pick[chosen, column, order_index] // 2
    first_expert = chosen * EXP_GROUP + hot_order[chosen, first_rank]
    second_expert = chosen * EXP_GROUP + hot_order[chosen, second_rank]
    joined = jnp.stack([first_expert, second_expert], axis=-1)
    return joined.reshape(N_GROUP * N_LOCAL * TOK_DEV, 2 * TOPG).astype(jnp.int32)


def steps_of(own_key, dims, cuts, least, largest):
    gain = 1.0
    for position, blocks in cuts:
        draws = jax.random.uniform(jax.random.fold_in(jax.random.fold_in(own_key, 6), position), (blocks,), jnp.float32, least / len(cuts), largest / len(cuts))
        gain = gain * jnp.repeat(jnp.exp(draws), dims[position] // blocks).reshape((-1,) + (1,) * (len(dims) - 1 - position))
    return gain


def normal_values(key, extent, deviation, bound, cuts=(), held_as=jnp.bfloat16):
    loudness = steps_of(key, extent, cuts, -0.22, 0.18) if cuts else 1.0
    array = jax.random.normal(key, extent, jnp.float32) * deviation * loudness
    return jnp.minimum(jnp.maximum(array, -bound), bound).astype(held_as)


def setup_inputs(seed: int = 0) -> dict:
    key_list = jax.random.split(jax.random.key(seed), 9)
    return {
        "grad_out": normal_values(key_list[0], (TOKENS, D), 1.0, 6.0, ((0, 1024),)),
        "routes": draw_routes(jax.random.fold_in(key_list[8], 71), 0),
        "router_weights": jnp.clip(jax.random.uniform(key_list[2], (TOKENS, TOPK), jnp.float32, 0.05, 0.5), 0.05, 0.5),
        "gate_weight": normal_values(key_list[3], (DEVICES, D, HID_DEV), D ** -0.5, 0.09375, ((0, 1024),)),
        "up_weight": normal_values(key_list[4], (DEVICES, D, HID_DEV), D ** -0.5, 0.09375, ((0, 1024),)),
        "down_weight": normal_values(key_list[5], (DEVICES, HID_DEV, D), HID ** -0.5, 0.1875, ((0, 1024),)),
        "saved_gate": normal_values(key_list[6], (DEVICES, SLOTS, HID_DEV), 1.0, 6.0, ((0, 1024),)),
        "saved_up": normal_values(key_list[7], (DEVICES, SLOTS, HID_DEV), 1.0, 6.0, ((0, 1024),)),
    }


def expert_backward(expert_rows, w_gate, w_up, w_down, pre_gate, pre_up):
    contract = (((1,), (1,)), ((), ()))
    act_grad = lax.dot_general(expert_rows, w_down, contract, preferred_element_type=jnp.float32)
    gate_val = pre_gate.astype(jnp.float32)
    up_projection_value = pre_up.astype(jnp.float32)
    sigma = jax.nn.sigmoid(gate_val)
    active = gate_val * sigma
    gate_part = jnp.sum(active * up_projection_value * act_grad, axis=1).astype(jnp.bfloat16)
    grad_gate_pre = (act_grad * up_projection_value * sigma * (1.0 + gate_val * (1.0 - sigma))).astype(jnp.bfloat16)
    grad_up_pre = (act_grad * active).astype(jnp.bfloat16)
    partial_in = lax.dot_general(grad_gate_pre, w_gate, contract, preferred_element_type=jnp.float32)
    partial_in = partial_in + lax.dot_general(grad_up_pre, w_up, contract, preferred_element_type=jnp.float32)
    return partial_in.astype(jnp.bfloat16), gate_part


def slot_tables(route_columns, expert):
    named_route = route_columns == expert
    is_named = jnp.any(named_route, axis=2)
    slot_order = jnp.cumsum(is_named.astype(jnp.int32), axis=1) - 1
    slot_ids = jnp.arange(CAP, dtype=jnp.int32)
    onehot = is_named[:, None, :] & (slot_order[:, None, :] == slot_ids[None, :, None])
    return onehot.astype(jnp.float32), named_route.astype(jnp.float32)


def reference(grad_out, routes, router_weights, gate_weight, up_weight, down_weight, saved_gate, saved_up):
    col_tokens = N_GROUP * TOK_DEV
    highest = lax.Precision.HIGHEST

    def by_column(table):
        last = table.shape[-1]
        return jnp.swapaxes(table.reshape(N_GROUP, N_LOCAL, TOK_DEV, last), 0, 1).reshape(N_LOCAL, col_tokens, last)

    def per_group(table):
        return table.reshape((N_GROUP, N_LOCAL) + table.shape[1:])

    route_columns = by_column(routes)
    weight_cols = by_column(router_weights)
    grad_cols = by_column(grad_out).astype(jnp.float32)

    def group_step(carry, inputs):
        total_in, total_gate = carry
        group_index, w_gate, w_up, w_down, pre_gate, pre_up = inputs

        def device_step(acc, dev_inputs):
            acc_in, acc_gate = acc
            resident_index, dev_gate, dev_up, dev_down, dev_pre_gate, dev_pre_up = dev_inputs
            expert = group_index * EXP_GROUP + resident_index // HSPLIT
            onehot, named_route = slot_tables(route_columns, expert)
            expert_rows = jnp.einsum('lcr,lrf->lcf', onehot, grad_cols, precision=highest)
            expert_rows = expert_rows.astype(jnp.bfloat16).reshape(SLOTS, D)
            partial_in, gate_part = expert_backward(expert_rows, dev_gate, dev_up, dev_down, dev_pre_gate, dev_pre_up)
            route_weight = jnp.sum(named_route * weight_cols, axis=2)
            acc_in = acc_in + jnp.einsum('lcr,lcf->lrf', onehot * route_weight[:, None, :],
                                         partial_in.astype(jnp.float32).reshape(N_LOCAL, CAP, D), precision=highest)
            acc_gate = acc_gate + jnp.einsum('lcr,lrk,lc->lrk', onehot, named_route,
                                             gate_part.astype(jnp.float32).reshape(N_LOCAL, CAP), precision=highest)
            return (acc_in, acc_gate), None

        start = (jnp.zeros((N_LOCAL, col_tokens, D), jnp.float32), jnp.zeros((N_LOCAL, col_tokens, TOPK), jnp.float32))
        local_ids = jnp.arange(N_LOCAL, dtype=jnp.int32)
        (acc_in, acc_gate), _ = lax.scan(device_step, start, (local_ids, w_gate, w_up, w_down, pre_gate, pre_up))
        rounded_input = lax.optimization_barrier(acc_in.astype(jnp.bfloat16))
        rounded_gate = lax.optimization_barrier(acc_gate.astype(jnp.bfloat16))
        total_in = total_in + rounded_input.astype(jnp.float32)
        total_gate = total_gate + rounded_gate.astype(jnp.float32)
        return (total_in, total_gate), None

    start = (jnp.zeros((N_LOCAL, col_tokens, D), jnp.float32), jnp.zeros((N_LOCAL, col_tokens, TOPK), jnp.float32))
    group_ids = jnp.arange(N_GROUP, dtype=jnp.int32)
    (total_in, total_gate), _ = lax.scan(group_step, start, (group_ids, per_group(gate_weight), per_group(up_weight),
                                                           per_group(down_weight), per_group(saved_gate), per_group(saved_up)))

    def to_tokens(table):
        last = table.shape[-1]
        return jnp.swapaxes(table.reshape(N_LOCAL, N_GROUP, TOK_DEV, last), 0, 1).reshape(TOKENS, last)

    grad_in = to_tokens(total_in).astype(jnp.bfloat16)
    grad_gate = to_tokens(total_gate).astype(jnp.bfloat16)
    return (grad_in, grad_gate)
```

```python
import functools

import jax
import jax.numpy as jnp
from jax import lax
from jax.experimental import pallas as pl
from jax.experimental.pallas import tpu as pltpu
from jax.sharding import PartitionSpec as P

MESH = pl.DeviceIdType.MESH
EXP_GROUP = 8
CAP = 4
LIVE = 8
LANES = 128
F32 = jnp.float32
BF16 = jnp.bfloat16


def iota(shape, dim):
    return lax.broadcasted_iota(jnp.int32, shape, dim)


def one(mask):
    return jnp.where(mask, 1.0, 0.0)


def dot(a, b):
    return jnp.dot(a, b, preferred_element_type=F32)


def dot_nt(a, b):
    return lax.dot_general(a, b, (((1,), (1,)), ((), ())), preferred_element_type=F32)


def split_columns(width, parts):
    tiles = width // LANES
    sizes = [(tiles // parts + (i < tiles % parts)) * LANES for i in range(parts)]
    starts = [sum(sizes[:i]) for i in range(parts)]
    return list(zip(starts, sizes))


def kernel(dims, grad, routes_t, weights_t, s_gate, s_up, w_gate, w_up, w_down, grad_in, grad_gate, *scratch):
    n_group, n_z, n_xh, tok, topk, D, n_split, parts_in, parts_out = dims
    n_local = n_z * n_xh
    plane = n_group * n_xh
    rows_z = n_xh * LIVE
    rows = n_z * rows_z
    cut_in = split_columns(D, parts_in)
    cut_out = split_columns(D + LANES, parts_out)
    it = iter(scratch)
    take = lambda n: [next(it) for _ in range(n)]
    plane_recv, gathered, w_cat, w_dn, f_gate, f_up, f_part, k_mat, w_rep, pick, table, plane_send, final_recv = take(13)
    blocks = take(parts_in)
    mine = take(parts_out)
    from_left = take(parts_out)
    from_right = take(parts_out)
    (own_sem, w_sem, ps_sem, pr_sem, fs_sem, fr_sem, gs_r, gr_r, gs_l, gr_l, ss_r, sr_r, ss_l, sr_l) = take(14)

    g = lax.axis_index("group")
    m = lax.axis_index("local")
    z = m // n_xh
    xh = lax.rem(m, n_xh)
    me = g * n_xh + xh
    right = (g, lax.rem(m + n_xh, n_local))
    left = (g, lax.rem(m + n_local - n_xh, n_local))
    expert = g * EXP_GROUP + m // n_split

    def peer(d):
        p = lax.rem(me + d, plane)
        return p, (p // n_xh, z * n_xh + lax.rem(p, n_xh))

    def zmod(v):
        return lax.rem(v + 2 * n_z, n_z)

    w_copies = [
        pltpu.make_async_copy(w_down, w_dn, w_sem.at[0]),
        pltpu.make_async_copy(w_gate, w_cat.at[:, pl.ds(0, LANES)], w_sem.at[1]),
        pltpu.make_async_copy(w_up, w_cat.at[:, pl.ds(LANES, LANES)], w_sem.at[2]),
    ]
    for copy in w_copies:
        copy.start()
    own = pltpu.make_async_copy(grad, plane_recv.at[me], own_sem.at[0])
    own.start()

    barrier = pltpu.get_barrier_semaphore()
    for d in range(1, plane):
        pl.semaphore_signal(barrier, inc=1, device_id=peer(d)[1], device_id_type=MESH)
    for side in (left, right):
        pl.semaphore_signal(barrier, inc=1, device_id=side, device_id_type=MESH)
    pl.semaphore_wait(barrier, plane + 1)

    def plane_copy(d):
        _, dev = peer(d)
        return pltpu.make_async_remote_copy(
            grad, plane_recv.at[me], ps_sem.at[d], pr_sem.at[me], device_id=dev, device_id_type=MESH
        )

    for d in range(1, plane):
        plane_copy(d).start()

    q_pad = 8
    a_id = lambda shape, dim: iota(shape, dim) // 8
    lane_r, lane_c = iota((LANES, LANES), 0), iota((LANES, LANES), 1)
    pair = one(lane_r // tok == lane_c // tok).astype(BF16)
    earlier = one((lane_r // tok == lane_c // tok) & (lane_r < lane_c)).astype(BF16)
    before = one(lane_c // 8 < lane_r // 8).astype(BF16)
    same = one(lane_c // 8 == lane_r // 8).astype(BF16)

    stacked = jnp.concatenate([routes_t[:, pl.ds(a * LANES, LANES)] for a in range(n_group)], axis=0)
    weight = jnp.concatenate([weights_t[:, pl.ds(a * LANES, LANES)] for a in range(n_group)], axis=0)
    in_group = one(stacked // EXP_GROUP == g)
    is_mine = one(stacked == expert)

    def ordered(hits):
        h = hits.astype(BF16)
        total = dot(h, pair).astype(BF16)
        previous = dot(h, earlier).astype(BF16)
        return dot(before, total) + dot(same, previous), dot(same, h)

    group_pos, group_hit = ordered(in_group)
    slot_pos, mine_hit = ordered(is_mine)
    j_id = lax.rem(lane_r, 8)
    placed = (group_hit > 0.5) & (group_pos == (2 * j_id).astype(F32))
    placed_f = one(placed)
    q_id = lax.rem(lane_c, q_pad)
    spread = one((lane_r == z * n_xh * tok + q_id) & (q_id < n_xh * tok)).astype(BF16)
    sent = dot(placed_f.astype(BF16), spread) * one(lane_r // 8 == lane_c // q_pad)
    folded = sum(sent[a * 8 : a * 8 + 8] for a in range(n_group))
    q8 = lax.rem(iota((8, LANES), 1), q_pad)
    pick_f = jnp.concatenate([jnp.where(q8 // tok == x, folded, 0.0) for x in range(n_xh)], axis=0)
    pick[...] = pick_f

    gathered[...] = jnp.zeros_like(gathered)
    own.wait()
    for d in range(1, plane):
        p, dev = peer(d)
        pltpu.make_async_remote_copy(
            grad, plane_recv.at[p], ps_sem.at[d], pr_sem.at[p], device_id=dev, device_id_type=MESH
        ).wait_recv()
    for a in range(n_group):
        for x in range(n_xh):
            gathered[pl.ds(a * q_pad + x * tok, tok), :] = plane_recv[a * n_xh + x].astype(F32)
    pick_b = pick_f.astype(BF16)
    for (start, size), block in zip(cut_in, blocks):
        block[z] = dot(pick_b, gathered[:, pl.ds(start, size)].astype(BF16)).astype(BF16)

    steps_r, steps_l = n_z // 2, n_z - 1 - n_z // 2

    def gather_copy(side, step, c):
        to_right = side == 0
        which = zmod(z - step) if to_right else zmod(z + step)
        return pltpu.make_async_remote_copy(
            blocks[c].at[which],
            blocks[c].at[which],
            (gs_r if to_right else gs_l).at[step, c],
            (gr_r if to_right else gr_l).at[step, c],
            device_id=right if to_right else left,
            device_id_type=MESH,
        )

    def gather_arrived(side, step, c):
        to_right = side == 0
        which = zmod(z - step - 1) if to_right else zmod(z + step + 1)
        pltpu.make_async_remote_copy(
            blocks[c].at[which],
            blocks[c].at[which],
            (gs_r if to_right else gs_l).at[step, c],
            (gr_r if to_right else gr_l).at[step, c],
            device_id=right if to_right else left,
            device_id_type=MESH,
        ).wait_recv()

    def gather_step(step):
        for c in range(parts_in):
            for side, count in ((0, steps_r), (1, steps_l)):
                if step < count:
                    if step:
                        gather_arrived(side, step - 1, c)
                    gather_copy(side, step, c).start()

    def tables():
        blocks_of = lambda v: [v[a * 8 : a * 8 + 8] for a in range(n_group)]
        fold = lambda v: sum(blocks_of(v))
        parts = [fold(placed_f * one((mine_hit > 0.5) & (slot_pos == float(c)))) for c in range(CAP)]
        for k in range(topk):
            parts.append(
                sum(placed_f[a * 8 : a * 8 + 8] * is_mine[a * 8 + k : a * 8 + k + 1] for a in range(n_group))
            )
        named = is_mine * weight
        w_all = sum(
            placed_f[a * 8 : a * 8 + 8] * jnp.sum(named[a * 8 : a * 8 + 8], axis=0, keepdims=True)
            for a in range(n_group)
        )
        w_hi = w_all.astype(BF16).astype(F32)
        w_mid = (w_all - w_hi).astype(BF16).astype(F32)
        parts += [w_hi, w_mid, w_all - w_hi - w_mid, jnp.zeros((8, LANES), F32)]
        stack = jnp.concatenate(parts, axis=0).astype(BF16)
        row, lane = iota((rows, LANES), 0), iota((rows, LANES), 1)
        expand = one(lane // tok == row // LIVE).astype(BF16)
        spread_out = dot_nt(expand, stack) * one(lax.rem(lane, 8) == lax.rem(row, 8))
        table[...] = spread_out.astype(BF16)

    def factors():
        slots = n_local * CAP
        x_id = lambda n: iota((LANES, n), 0) // 8
        t = table[...]
        to_slot = one(x_id(slots) == lax.rem(iota((LANES, slots), 1), CAP)).astype(BF16)
        to_k = one(x_id(LANES) - CAP == iota((LANES, LANES), 1)).astype(BF16)
        to_k = to_k * one(x_id(LANES) < CAP + topk).astype(BF16)
        to_w = one((x_id(LANES) >= CAP + topk) & (x_id(LANES) < CAP + topk + 3)).astype(BF16)
        k_mat[...] = dot(t, to_k)
        w_rep[...] = dot(t, to_w)
        member = dot(t, to_slot) * one(
            iota((rows, slots), 0) // LIVE == iota((rows, slots), 1) // CAP
        )
        member = member.astype(BF16)
        p = dot(member, s_gate[...])
        q = dot(member, s_up[...])
        sigma = jax.nn.sigmoid(p)
        active = p * sigma
        f_gate[...] = q * sigma * (1.0 + p * (1.0 - sigma))
        f_up[...] = active
        f_part[...] = active * q

    for step in range(steps_r):
        gather_step(step)
        if step == 1:
            tables()
        if step == 2:
            factors()
    for c in range(parts_in):
        gather_arrived(0, steps_r - 1, c)
        gather_arrived(1, steps_l - 1, c)

    for copy in w_copies:
        copy.wait()
    act = sum(
        dot_nt(block[...].reshape(rows, size), w_dn[:, pl.ds(start, size)])
        for (start, size), block in zip(cut_in, blocks)
    )
    part = jnp.sum(f_part[...] * act, axis=1, keepdims=True) * k_mat[...]
    pre = jnp.concatenate([(act * f_gate[...]).astype(BF16), (act * f_up[...]).astype(BF16)], axis=1)
    table[...] = part.astype(BF16)
    f_gate[...] = pre[:, :LANES].astype(F32)
    f_up[...] = pre[:, LANES:].astype(F32)

    tile = 4
    tile_rows = tile * rows_z

    @pl.loop(0, n_z // tile)
    def _(i):
        at = pl.ds(pl.multiple_of(i * tile_rows, tile_rows), tile_rows)
        both = jnp.concatenate([f_gate[at, :].astype(BF16), f_up[at, :].astype(BF16)], axis=1)
        w = w_rep[at, :][:, 0:1]
        for (start, size), out in zip(cut_out, mine):
            end = min(start + size, D)
            value = (dot_nt(both, w_cat[pl.ds(start, end - start), :]) * w).astype(BF16)
            out[pl.ds(i * tile, tile), :, pl.ds(0, end - start)] = value.reshape(tile, rows_z, end - start)
            if start + size > D:
                gate = table[at, :].reshape(tile, rows_z, LANES)
                out[pl.ds(i * tile, tile), :, pl.ds(end - start, LANES)] = gate

    def sum_copy(side, step, c, src):
        to_right = side == 0
        return pltpu.make_async_remote_copy(
            src,
            (from_left if to_right else from_right)[c].at[step],
            (ss_r if to_right else ss_l).at[step, c],
            (sr_r if to_right else sr_l).at[step, c],
            device_id=right if to_right else left,
            device_id_type=MESH,
        )

    def sum_step(step):
        for c in range(parts_out):
            for side, count in ((0, steps_r), (1, steps_l)):
                if step < count:
                    held = (from_left if side == 0 else from_right)[c]
                    which = zmod(z + steps_r - step) if side == 0 else zmod(z - steps_l + step)
                    src = mine[c].at[which]
                    if step:
                        sum_copy(side, step - 1, c, src).wait_recv()
                        src = held.at[step - 1]
                        src[...] = (src[...].astype(F32) + mine[c][which].astype(F32)).astype(BF16)
                    sum_copy(side, step, c, src).start()

    for step in range(steps_r):
        sum_step(step)

    for c, (start, size) in enumerate(cut_out):
        sum_copy(0, steps_r - 1, c, mine[c].at[z]).wait_recv()
        sum_copy(1, steps_l - 1, c, mine[c].at[z]).wait_recv()
        total = mine[c][z].astype(F32) + from_left[c][steps_r - 1].astype(F32) + from_right[c][steps_l - 1].astype(F32)
        back = lax.dot_general(
            pick[...].astype(BF16), total.astype(BF16), (((0,), (0,)), ((), ())), preferred_element_type=F32
        )
        for a in range(n_group):
            for x in range(n_xh):
                at = a * q_pad + x * tok
                plane_send[a * n_xh + x, :, pl.ds(start, size)] = back[at : at + tok].astype(BF16)

    def final_copy(d):
        p, dev = peer(d)
        return pltpu.make_async_remote_copy(
            plane_send.at[p], final_recv.at[me], fs_sem.at[d], fr_sem.at[me], device_id=dev, device_id_type=MESH
        )

    own_final = pltpu.make_async_copy(plane_send.at[me], final_recv.at[me], own_sem.at[1])
    own_final.start()
    for d in range(1, plane):
        final_copy(d).start()

    for d in range(1, plane):
        plane_copy(d).wait_send()
    for step in range(steps_r):
        for side, count in ((0, steps_r), (1, steps_l)):
            if step < count:
                for c in range(parts_in):
                    gather_copy(side, step, c).wait_send()
                for c in range(parts_out):
                    sum_copy(side, step, c, mine[c].at[z]).wait_send()

    own_final.wait()
    for d in range(1, plane):
        p, dev = peer(d)
        pltpu.make_async_remote_copy(
            plane_send.at[p], final_recv.at[p], fs_sem.at[d], fr_sem.at[p], device_id=dev, device_id_type=MESH
        ).wait_recv()
    total = final_recv[0].astype(F32)
    for p in range(1, plane):
        total = total + final_recv[p].astype(F32)
    grad_in[...] = total[:, :D].astype(BF16)
    grad_gate[...] = total[:, D:].astype(BF16)
    for d in range(1, plane):
        final_copy(d).wait_send()


def local(n_group, n_local, grad_out, routes, router_weights, gate_weight, up_weight, down_weight, saved_gate, saved_up):
    tok, D = grad_out.shape
    topk = routes.shape[1]
    hid = saved_gate.shape[2]
    n_xh = 2
    n_z = n_local // n_xh
    n_split = n_local // EXP_GROUP
    parts_in = parts_out = 2
    plane = n_group * n_xh
    rows_z = n_xh * LIVE
    rows = n_z * rows_z
    wide = D + LANES
    cut_in, cut_out = split_columns(D, parts_in), split_columns(wide, parts_out)
    steps_r, steps_l = n_z // 2, n_z - 1 - n_z // 2
    dims = (n_group, n_z, n_xh, tok, topk, D, n_split, parts_in, parts_out)
    vmem = pl.BlockSpec(memory_space=pltpu.VMEM)
    hbm = pl.BlockSpec(memory_space=pl.ANY)
    dma = lambda *shape: pltpu.SemaphoreType.DMA(shape)
    scratch = [
        pltpu.VMEM((plane, tok, D), BF16),
        pltpu.VMEM((n_group * 8, D), F32),
        pltpu.VMEM((D, 2 * hid), BF16),
        pltpu.VMEM((hid, D), BF16),
        pltpu.VMEM((rows, hid), F32),
        pltpu.VMEM((rows, hid), F32),
        pltpu.VMEM((rows, hid), F32),
        pltpu.VMEM((rows, LANES), F32),
        pltpu.VMEM((rows, LANES), F32),
        pltpu.VMEM((rows_z, LANES), F32),
        pltpu.VMEM((rows, LANES), BF16),
        pltpu.VMEM((plane, tok, wide), BF16),
        pltpu.VMEM((plane, tok, wide), BF16),
    ]
    scratch += [pltpu.VMEM((n_z, rows_z, size), BF16) for _, size in cut_in]
    scratch += [pltpu.VMEM((n_z, rows_z, size), BF16) for _, size in cut_out]
    scratch += [pltpu.VMEM((steps_r, rows_z, size), BF16) for _, size in cut_out]
    scratch += [pltpu.VMEM((steps_l, rows_z, size), BF16) for _, size in cut_out]
    scratch += [dma(2), dma(3), dma(plane), dma(plane), dma(plane), dma(plane)]
    scratch += [dma(steps_r, parts_in)] * 2 + [dma(steps_l, parts_in)] * 2
    scratch += [dma(steps_r, parts_out)] * 2 + [dma(steps_l, parts_out)] * 2
    grad_in, gate = pl.pallas_call(
        functools.partial(kernel, dims),
        out_shape=(
            jax.ShapeDtypeStruct((tok, D), BF16),
            jax.ShapeDtypeStruct((tok, LANES), BF16),
        ),
        in_specs=[vmem] * 5 + [hbm] * 3,
        out_specs=(vmem, vmem),
        scratch_shapes=scratch,
        compiler_params=pltpu.CompilerParams(
            collective_id=0, has_side_effects=True, vmem_limit_bytes=56 * 1024 * 1024
        ),
        cost_estimate=pl.CostEstimate(
            flops=6 * rows * D * hid, bytes_accessed=3 * 2 * D * hid, transcendentals=rows * hid
        ),
    )(grad_out, routes.T, router_weights.T, saved_gate[0], saved_up[0], gate_weight[0], up_weight[0], down_weight[0])
    return grad_in, gate[:, :topk]


def solution(mesh):
    rows = P(("group", "local"), None)
    whole = P(("group", "local"), None, None)
    return jax.shard_map(
        functools.partial(local, mesh.shape["group"], mesh.shape["local"]),
        mesh=mesh,
        in_specs=(rows, P(), P(), whole, whole, whole, whole, whole),
        out_specs=(rows, rows),
        check_vma=False,
    )
```

```python
import functools

import jax
import jax.numpy as jnp
from jax import lax
from jax.experimental import pallas as pl
from jax.experimental.pallas import tpu as pltpu
from jax.sharding import PartitionSpec as P

MESH = pl.DeviceIdType.MESH
EXP_GROUP = 8
CAP = 4
QUARTERS = 4
LANES = 128
F32 = jnp.float32
BF16 = jnp.bfloat16


def iota(shape, dim):
    return lax.broadcasted_iota(jnp.int32, shape, dim)


def one(mask):
    return jnp.where(mask, 1.0, 0.0)


def dot(a, b):
    return jnp.dot(a, b, preferred_element_type=F32)


def dot_nt(a, b):
    return lax.dot_general(a, b, (((1,), (1,)), ((), ())), preferred_element_type=F32)


def dot_tn(a, b):
    return lax.dot_general(a, b, (((0,), (0,)), ((), ())), preferred_element_type=F32)


def offset_of(n):
    return (n + 1) // 2 if n % 2 else -(n // 2)


def kernel(dims, grad, routes_t, weights_t, s_gate, s_up, w_gate, w_up, w_down, grad_in, grad_gate, *scratch):
    n_group, n_z, n_xh, tok, topk, D = dims
    n_local = n_z * n_xh
    n_block = EXP_GROUP
    line = n_z // n_block
    part = D // QUARTERS
    wide = part + LANES
    tall = QUARTERS * CAP
    rows = n_local * tall
    (
        plane_recv, gathered, w_cat, w_dn, f_gate, f_up, f_part, slots, x_buf, y_buf, pair_sum,
        from_left, from_right, total, closing, home, plane_send, final_recv,
        own_sem, w_sem, ps_sem, pr_sem, fs_sem, fr_sem, far_s, far_r, right_s, left_s, line_r, pair_s, pair_r,
        add_s, add_r, up_s, up_r, down_s, down_r, home_s, home_r,
    ) = scratch

    g = lax.axis_index("group")
    m = lax.axis_index("local")
    z = m // n_xh
    xh = lax.rem(m, n_xh)
    other = 1 - xh
    zb = z // line
    r = lax.rem(z, line)
    right = (g, lax.rem(m + n_xh, n_local))
    left = (g, lax.rem(m + n_local - n_xh, n_local))
    pair = (g, z * n_xh + other)

    def block_at(offset):
        return lax.rem(zb + offset + n_block, n_block)

    def far(offset):
        return (g, (block_at(offset) * line + r) * n_xh + xh)

    def peer(d):
        p = lax.rem(g + d, n_group)
        return p, (p, m)

    def remote(src, dst, send, recv, dev):
        return pltpu.make_async_remote_copy(src, dst, send, recv, device_id=dev, device_id_type=MESH)

    w_copies = []
    for q in range(QUARTERS):
        cols = pl.ds(q * part, part)
        w_copies += [
            pltpu.make_async_copy(w_down.at[:, cols], w_dn.at[pl.ds(q * LANES, LANES), :], w_sem.at[q, 0]),
            pltpu.make_async_copy(w_gate.at[cols, :], w_cat.at[:, pl.ds(2 * q * LANES, LANES)], w_sem.at[q, 1]),
            pltpu.make_async_copy(w_up.at[cols, :], w_cat.at[:, pl.ds((2 * q + 1) * LANES, LANES)], w_sem.at[q, 2]),
        ]
    own = pltpu.make_async_copy(grad, plane_recv.at[g], own_sem.at[0])
    own.start()

    barrier = pltpu.get_barrier_semaphore()
    greeted = [peer(d)[1] for d in range(1, n_group)] + [left, right, pair]
    greeted += [far(offset_of(n)) for n in range(1, n_block)]
    for dev in greeted:
        pl.semaphore_signal(barrier, inc=1, device_id=dev, device_id_type=MESH)
    pl.semaphore_wait(barrier, len(greeted))

    def plane_copy(d):
        return remote(grad, plane_recv.at[g], ps_sem.at[d], pr_sem.at[g], peer(d)[1])

    for d in range(1, n_group):
        plane_copy(d).start()
    for copy in w_copies:
        copy.start()

    lane_r, lane_c = iota((LANES, LANES), 0), iota((LANES, LANES), 1)
    stacked = jnp.concatenate([routes_t[:, pl.ds(a * LANES, LANES)] for a in range(n_group)], axis=0)
    weight = jnp.concatenate([weights_t[:, pl.ds(a * LANES, LANES)] for a in range(n_group)], axis=0)
    t_id = lax.rem(lane_c, 8)
    spread = one((lane_r == m * tok + t_id) & (t_id < tok)).astype(BF16)
    source = one(lane_r // 8 == lane_c // 8)

    def fold(v):
        v = v * source
        return sum(v[a * 8 : a * 8 + 8] for a in range(n_group))

    hi = weight.astype(BF16)
    mid = (weight - hi.astype(F32)).astype(BF16)
    low = (weight - hi.astype(F32) - mid.astype(F32)).astype(BF16)
    own_routes = fold(dot(stacked.astype(F32).astype(BF16), spread))
    own_weights = fold(dot(hi, spread) + dot(mid, spread) + dot(low, spread))
    valid = lax.rem(iota((8, LANES), 1), 8) < tok
    own_routes = jnp.where(valid, own_routes, -1.0)
    first = (g * EXP_GROUP).astype(F32)
    hits, hit_w = [], []
    for e in range(EXP_GROUP):
        same = one(own_routes == first + float(e))
        hits.append(jnp.sum(same, axis=0, keepdims=True))
        hit_w.append(jnp.sum(same * own_weights, axis=0, keepdims=True))
    widen = lambda v: jnp.concatenate([jnp.broadcast_to(t, (tall, LANES)) for t in v], axis=0)
    hit = widen(hits)
    order = dot(hit.astype(BF16), one(lane_r < lane_c).astype(BF16))
    table = hit * one(order == lax.rem(lane_r, CAP).astype(F32))
    quarter = lax.rem(lane_r, tall) // CAP
    slot_weight = jnp.sum(table * widen(hit_w), axis=1, keepdims=True)
    padded = jnp.concatenate([own_routes, jnp.full((LANES - topk, LANES), -1.0, F32)], axis=0)
    slot_routes = dot_nt(table.astype(BF16), padded.astype(BF16))
    which_k = one((slot_routes == first + (lane_r // tall).astype(F32)) & (lane_c < topk))
    tables = [(table * one(quarter == q)).astype(BF16) for q in range(QUARTERS)]

    gathered[...] = jnp.zeros_like(gathered)
    own.wait()
    for d in range(1, n_group):
        p, dev = peer(d)
        remote(grad, plane_recv.at[p], ps_sem.at[d], pr_sem.at[p], dev).wait_recv()
    for a in range(n_group):
        gathered[pl.ds(a * 8, tok), :] = plane_recv[a].astype(F32)
    slot_rows = sum(
        dot(tables[q], gathered[:, pl.ds(q * part, part)].astype(BF16)) for q in range(QUARTERS)
    ).astype(BF16)
    slots[...] = slot_rows.reshape(n_block, tall, part)

    def far_copy(n):
        to = block_at(-offset_of(n))
        return remote(slots.at[to], x_buf.at[xh, n, r], far_s.at[n], far_r.at[n], far(-offset_of(n)))

    for n in range(n_block - 1, 0, -1):
        far_copy(n).start()
    x_buf[xh, 0, r] = slots[zb]

    def along(n, k, to_right):
        at = x_buf.at[xh, n, k]
        if to_right:
            return remote(at, at, right_s.at[n, k], line_r.at[n, k], right)
        return remote(at, at, left_s.at[n, k], line_r.at[n, k], left)

    def across(n, k):
        at = x_buf.at[xh, n, k]
        return remote(at, at, pair_s.at[n, k], pair_r.at[n, k], pair)

    def when(condition, action):
        pl.when(condition)(action)

    def pass_on(n, d, to_right):
        k = r - d if to_right else r + d

        def arrived():
            along(n, k, to_right).wait_recv()
            when(r < line - 1 if to_right else r > 0, lambda: along(n, k, to_right).start())
            across(n, k).start()

        when(r >= d if to_right else r + d <= line - 1, arrived)

    def factors():
        tile = 8 * tall

        @pl.loop(0, rows // tile)
        def _(i):
            row = iota((tile, n_local * CAP), 0) + i * tile
            slot = iota((tile, n_local * CAP), 1)
            n = lax.rem(row // (line * tall), n_block)
            offset = jnp.where(lax.rem(n, 2) == 1, (n + 1) // 2, -(n // 2))
            block = lax.rem(zb + offset + n_block, n_block)
            index = (block * line + lax.rem(row // tall, line)) * n_xh + row // (n_block * line * tall)
            member = one(slot == index * CAP + lax.rem(row, CAP)).astype(BF16)
            p = dot(member, s_gate[...])
            q = dot(member, s_up[...])
            sigma = jax.nn.sigmoid(p)
            active = p * sigma
            at = pl.ds(pl.multiple_of(i * tile, tile), tile)
            f_gate[at, :] = q * sigma * (1.0 + p * (1.0 - sigma))
            f_up[at, :] = active
            f_part[at, :] = active * q

    for step in range(n_block + line - 1):
        if step < n_block:
            if step:
                far_copy(step).wait_recv()
            when(r < line - 1, lambda: along(step, r, True).start())
            when(r > 0, lambda: along(step, r, False).start())
            across(step, r).start()
        if step == 0:
            factors()
        for d in range(1, line):
            if 0 <= step - d < n_block:
                pass_on(step - d, d, True)
                pass_on(step - d, d, False)

    for copy in w_copies:
        copy.wait()

    def compute(half, i):
        tile = 2 * line * tall
        row0 = pl.multiple_of((half * (n_block // 2) + i) * tile, tile)
        at = pl.ds(row0, tile)
        x = x_buf[half, pl.ds(2 * i, 2)].reshape(tile, part)
        each = dot_nt(x, w_dn[...])
        q_id = lax.rem(iota((tile, LANES), 0), tall) // CAP
        mine = sum(jnp.where(q_id == q, each[:, q * LANES : (q + 1) * LANES], 0.0) for q in range(QUARTERS))
        mine = mine.reshape(2 * line, 2, 8, LANES)
        mine = mine[:, 0] + mine[:, 1]
        mine = mine + pltpu.roll(mine, CAP, 1)
        act = jnp.stack([mine, mine], axis=1).reshape(tile, LANES)
        gate = jnp.sum(f_part[at, :] * act, axis=1, keepdims=True)
        gate_hi = gate.astype(BF16).astype(F32)
        gates = jnp.where(q_id == 0, gate_hi, jnp.where(q_id == 1, gate - gate_hi, 0.0)).astype(BF16)
        pre = [(act * f_gate[at, :]).astype(BF16), (act * f_up[at, :]).astype(BF16)]
        zero = jnp.zeros_like(pre[0])
        spread_pre = jnp.concatenate([jnp.where(q_id == q, v, zero) for q in range(QUARTERS) for v in pre], axis=1)
        out = dot_nt(spread_pre, w_cat[...]).astype(BF16)
        y_buf[half, pl.ds(2 * i, 2), :, :, pl.ds(0, part)] = out.reshape(2, line, tall, part)
        y_buf[half, pl.ds(2 * i, 2), :, :, pl.ds(part, LANES)] = gates.reshape(2, line, tall, LANES)

    def add_copy(n):
        return remote(y_buf.at[other, n], pair_sum.at[n], add_s.at[n], add_r.at[n], pair)

    for n in range(n_block):
        for k in range(line):
            at = x_buf.at[other, n, k]
            remote(at, at, pair_s.at[n, k], pair_r.at[n, k], pair).wait_recv()

    @pl.loop(0, n_block // 2)
    def _(j):
        i = n_block // 2 - 1 - j
        compute(other, i)
        add_copy(2 * i + 1).start()
        add_copy(2 * i).start()
        compute(xh, i)

    def sum_copy(n, k, to_right):
        src = y_buf.at[xh, n, k]
        if to_right:
            return remote(src, from_left.at[n, k], up_s.at[n, k], up_r.at[n, k], right)
        return remote(src, from_right.at[n, k], down_s.at[n, k], down_r.at[n, k], left)

    def gather_sum(n, k, sides):
        total[...] = y_buf[xh, n, k].astype(F32) + pair_sum[n, k].astype(F32)
        for to_right in sides:

            def add():
                sum_copy(n, k, to_right).wait_recv()
                total[...] += (from_left if to_right else from_right)[n, k].astype(F32)

            when(r > 0 if to_right else r < line - 1, add)

    def send_sum(step, d, to_right):
        p = step - r if to_right else step - (line - 1 - r)
        n = n_block - 1 - p
        k = r + d if to_right else r - d

        def go():
            gather_sum(n, k, (to_right,))
            y_buf[xh, n, k] = total[...].astype(BF16)
            sum_copy(n, k, to_right).start()

        inside = r + d <= line - 1 if to_right else r >= d
        when(inside & (p >= 0) & (p < n_block), go)

    def home_copy(n):
        return remote(closing.at[n], home.at[zb], home_s.at[n], home_r.at[zb], far(offset_of(n)))

    for step in range(n_block + line - 1):
        if step < n_block:
            add_copy(n_block - 1 - step).wait_recv()
        for d in range(line - 1, 0, -1):
            send_sum(step, d, True)
            send_sum(step, d, False)
        n = n_block - 1 - (step - (line - 1))
        if n < n_block:
            gather_sum(n, r, (True, False))
            if n:
                closing[n] = total[...].astype(BF16)
                home_copy(n).start()
            else:
                home[zb] = total[...].astype(BF16)

    for n in range(1, n_block):
        e = block_at(-offset_of(n))
        remote(closing.at[n], home.at[e], home_s.at[n], home_r.at[e], far(offset_of(n))).wait_recv()

    sums = home[...].reshape(n_block * tall, wide).astype(F32)
    weighted = sums[:, :part] * slot_weight
    w_hi = weighted.astype(BF16)
    w_low = (weighted - w_hi.astype(F32)).astype(BF16)
    for q in range(QUARTERS):
        back = (dot_tn(tables[q], w_hi) + dot_tn(tables[q], w_low)).astype(BF16).astype(F32)
        for a in range(n_group):
            plane_send[a, :, pl.ds(q * part, part)] = back[a * 8 : a * 8 + tok].astype(BF16)
    back = dot_tn(table.astype(BF16), (sums[:, part:] * which_k).astype(BF16))
    for a in range(n_group):
        plane_send[a, :, pl.ds(D, LANES)] = back[a * 8 : a * 8 + tok].astype(BF16)

    def final_copy(d):
        p, dev = peer(d)
        return remote(plane_send.at[p], final_recv.at[g], fs_sem.at[d], fr_sem.at[g], dev)

    own_final = pltpu.make_async_copy(plane_send.at[g], final_recv.at[g], own_sem.at[1])
    own_final.start()
    for d in range(1, n_group):
        final_copy(d).start()

    for d in range(1, n_group):
        plane_copy(d).wait_send()
    for n in range(n_block):
        if n:
            far_copy(n).wait_send()
            home_copy(n).wait_send()
        add_copy(n).wait_send()
        for k in range(line):
            across(n, k).wait_send()
            when((r < line - 1) & (k <= r), lambda: along(n, k, True).wait_send())
            when((r > 0) & (k >= r), lambda: along(n, k, False).wait_send())
            when(k > r, lambda: sum_copy(n, k, True).wait_send())
            when(k < r, lambda: sum_copy(n, k, False).wait_send())

    own_final.wait()
    for d in range(1, n_group):
        p, dev = peer(d)
        remote(plane_send.at[p], final_recv.at[p], fs_sem.at[d], fr_sem.at[p], dev).wait_recv()
    result = final_recv[0].astype(F32)
    for p in range(1, n_group):
        result = result + final_recv[p].astype(F32)
    grad_in[...] = result[:, :D].astype(BF16)
    grad_gate[...] = result[:, D:].astype(BF16)
    for d in range(1, n_group):
        final_copy(d).wait_send()


def local(n_group, n_local, grad_out, routes, router_weights, gate_weight, up_weight, down_weight, saved_gate, saved_up):
    tok, D = grad_out.shape
    topk = routes.shape[1]
    hid = saved_gate.shape[2]
    n_xh = 2
    n_z = n_local // n_xh
    n_block = EXP_GROUP
    line = n_z // n_block
    part = D // QUARTERS
    wide = part + LANES
    tall = QUARTERS * CAP
    rows = n_local * tall
    dims = (n_group, n_z, n_xh, tok, topk, D)
    vmem = pl.BlockSpec(memory_space=pltpu.VMEM)
    hbm = pl.BlockSpec(memory_space=pl.ANY)
    dma = lambda *shape: pltpu.SemaphoreType.DMA(shape)
    scratch = [
        pltpu.VMEM((n_group, tok, D), BF16),
        pltpu.VMEM((n_group * 8, D), F32),
        pltpu.VMEM((part, 2 * QUARTERS * hid), BF16),
        pltpu.VMEM((QUARTERS * hid, part), BF16),
        pltpu.VMEM((rows, hid), F32),
        pltpu.VMEM((rows, hid), F32),
        pltpu.VMEM((rows, hid), F32),
        pltpu.VMEM((n_block, tall, part), BF16),
        pltpu.VMEM((n_xh, n_block, line, tall, part), BF16),
        pltpu.VMEM((n_xh, n_block, line, tall, wide), BF16),
        pltpu.VMEM((n_block, line, tall, wide), BF16),
        pltpu.VMEM((n_block, line, tall, wide), BF16),
        pltpu.VMEM((n_block, line, tall, wide), BF16),
        pltpu.VMEM((tall, wide), F32),
        pltpu.VMEM((n_block, tall, wide), BF16),
        pltpu.VMEM((n_block, tall, wide), BF16),
        pltpu.VMEM((n_group, tok, D + LANES), BF16),
        pltpu.VMEM((n_group, tok, D + LANES), BF16),
    ]
    scratch += [dma(2), dma(QUARTERS, 3)] + [dma(n_group)] * 4 + [dma(n_block)] * 2
    scratch += [dma(n_block, line)] * 5 + [dma(n_block)] * 2 + [dma(n_block, line)] * 4 + [dma(n_block)] * 2
    grad_in, gate = pl.pallas_call(
        functools.partial(kernel, dims),
        out_shape=(
            jax.ShapeDtypeStruct((tok, D), BF16),
            jax.ShapeDtypeStruct((tok, LANES), BF16),
        ),
        in_specs=[vmem] * 5 + [hbm] * 3,
        out_specs=(vmem, vmem),
        scratch_shapes=scratch,
        compiler_params=pltpu.CompilerParams(
            collective_id=0, has_side_effects=True, vmem_limit_bytes=56 * 1024 * 1024
        ),
        cost_estimate=pl.CostEstimate(
            flops=6 * rows * D * hid, bytes_accessed=3 * 2 * D * hid, transcendentals=rows * hid
        ),
    )(grad_out, routes.T, router_weights.T, saved_gate[0], saved_up[0], gate_weight[0], up_weight[0], down_weight[0])
    return grad_in, gate[:, :topk]


def solution(mesh):
    rows = P(("group", "local"), None)
    whole = P(("group", "local"), None, None)
    return jax.shard_map(
        functools.partial(local, mesh.shape["group"], mesh.shape["local"]),
        mesh=mesh,
        in_specs=(rows, P(), P(), whole, whole, whole, whole, whole),
        out_specs=(rows, rows),
        check_vma=False,
    )
```

```python
import functools

import jax
import jax.numpy as jnp
from jax import lax
from jax.experimental import pallas as pl
from jax.experimental.pallas import tpu as pltpu
from jax.sharding import PartitionSpec as P

MESH = pl.DeviceIdType.MESH
EXP_GROUP = 8
CAP = 4
QUARTERS = 4
NEAR = 4
LANES = 128
F32 = jnp.float32
BF16 = jnp.bfloat16


def iota(shape, dim):
    return lax.broadcasted_iota(jnp.int32, shape, dim)


def one(mask):
    return jnp.where(mask, 1.0, 0.0)


def dot(a, b):
    return jnp.dot(a, b, preferred_element_type=F32)


def dot_nt(a, b):
    return lax.dot_general(a, b, (((1,), (1,)), ((), ())), preferred_element_type=F32)


def dot_tn(a, b):
    return lax.dot_general(a, b, (((0,), (0,)), ((), ())), preferred_element_type=F32)


def offset_of(n):
    half = lax.div(n + 1, 2)
    return jnp.where(lax.rem(n, 2) == 1, half, -half)


def kernel(dims, grad, routes_t, weights_t, s_gate, s_up, w_gate, w_up, w_down, grad_in, grad_gate, *scratch):
    n_group, n_z, n_xh, tok, topk, D = dims
    n_local = n_z * n_xh
    n_block = EXP_GROUP
    line = n_z // n_block
    part = D // QUARTERS
    wide = part + LANES
    tall = QUARTERS * CAP
    rows = n_local * tall
    (
        plane_recv, gathered, w_cat, w_dn, f_gate, f_up, f_part, slots, x_buf, y_buf, pair_sum,
        from_left, from_right, total, closing, home, plane_send, final_recv,
        own_sem, w_sem, ps_sem, pr_sem, fs_sem, fr_sem, far_s, far_r, right_s, left_s, line_r, pair_s, pair_r,
        add_s, add_r, up_s, up_r, down_s, down_r, home_s, home_r,
        relay_x, relay_h, leg_r, relay_s, home_leg_r, home_relay_s,
    ) = scratch

    g = lax.axis_index("group")
    m = lax.axis_index("local")
    z = m // n_xh
    xh = lax.rem(m, n_xh)
    other = 1 - xh
    zb = z // line
    r = lax.rem(z, line)
    right = (g, lax.rem(m + n_xh, n_local))
    left = (g, lax.rem(m + n_local - n_xh, n_local))
    pair = (g, z * n_xh + other)

    def block_at(offset):
        return lax.rem(zb + offset + n_block, n_block)

    def far(offset):
        return (g, (block_at(offset) * line + r) * n_xh + xh)

    def peer(d):
        p = lax.rem(g + d, n_group)
        return p, (p, m)

    def remote(src, dst, send, recv, dev):
        return pltpu.make_async_remote_copy(src, dst, send, recv, device_id=dev, device_id_type=MESH)

    w_copies = []
    for q in range(QUARTERS):
        cols = pl.ds(q * part, part)
        w_copies += [
            pltpu.make_async_copy(w_down.at[:, cols], w_dn.at[pl.ds(q * LANES, LANES), :], w_sem.at[q, 0]),
            pltpu.make_async_copy(w_gate.at[cols, :], w_cat.at[:, pl.ds(2 * q * LANES, LANES)], w_sem.at[q, 1]),
            pltpu.make_async_copy(w_up.at[cols, :], w_cat.at[:, pl.ds((2 * q + 1) * LANES, LANES)], w_sem.at[q, 2]),
        ]
    own = pltpu.make_async_copy(grad, plane_recv.at[g], own_sem.at[0])
    own.start()
    for copy in w_copies:
        copy.start()

    barrier = pltpu.get_barrier_semaphore()

    def greet(dev):
        pl.semaphore_signal(barrier, inc=1, device_id=dev, device_id_type=MESH)

    @pl.loop(1, NEAR + 1)
    def _(n):
        greet(far(offset_of(n)))

    @pl.loop(1, n_group)
    def _(d):
        greet(peer(d)[1])

    for dev in (left, right, pair):
        greet(dev)

    lane_r, lane_c = iota((LANES, LANES), 0), iota((LANES, LANES), 1)
    stacked = jnp.concatenate([routes_t[:, pl.ds(a * LANES, LANES)] for a in range(n_group)], axis=0)
    weight = jnp.concatenate([weights_t[:, pl.ds(a * LANES, LANES)] for a in range(n_group)], axis=0)
    t_id = lax.rem(lane_c, 8)
    spread = one((lane_r == m * tok + t_id) & (t_id < tok)).astype(BF16)
    source = one(lane_r // 8 == lane_c // 8)

    def fold(v):
        v = v * source
        return sum(v[a * 8 : a * 8 + 8] for a in range(n_group))

    hi = weight.astype(BF16)
    mid = (weight - hi.astype(F32)).astype(BF16)
    low = (weight - hi.astype(F32) - mid.astype(F32)).astype(BF16)
    own_routes = fold(dot(stacked.astype(F32).astype(BF16), spread))
    own_weights = fold(dot(hi, spread) + dot(mid, spread) + dot(low, spread))
    valid = lax.rem(iota((8, LANES), 1), 8) < tok
    own_routes = jnp.where(valid, own_routes, -1.0)
    first = (g * EXP_GROUP).astype(F32)
    hits, hit_w = [], []
    for e in range(EXP_GROUP):
        same = one(own_routes == first + float(e))
        hits.append(jnp.sum(same, axis=0, keepdims=True))
        hit_w.append(jnp.sum(same * own_weights, axis=0, keepdims=True))
    widen = lambda v: jnp.concatenate([jnp.broadcast_to(t, (tall, LANES)) for t in v], axis=0)
    hit = widen(hits)
    order = dot(hit.astype(BF16), one(lane_r < lane_c).astype(BF16))
    table = hit * one(order == lax.rem(lane_r, CAP).astype(F32))
    quarter = lax.rem(lane_r, tall) // CAP
    slot_weight = jnp.sum(table * widen(hit_w), axis=1, keepdims=True)
    padded = jnp.concatenate([own_routes, jnp.full((LANES - topk, LANES), -1.0, F32)], axis=0)
    slot_routes = dot_nt(table.astype(BF16), padded.astype(BF16))
    which_k = one((slot_routes == first + (lane_r // tall).astype(F32)) & (lane_c < topk))
    tables = [(table * one(quarter == q)).astype(BF16) for q in range(QUARTERS)]

    gathered[...] = jnp.zeros_like(gathered)

    f_tile = 8 * tall

    @pl.loop(0, rows // f_tile)
    def _(i):
        row = iota((f_tile, n_local * CAP), 0) + i * f_tile
        slot = iota((f_tile, n_local * CAP), 1)
        n = lax.rem(row // (line * tall), n_block)
        block = lax.rem(zb + offset_of(n) + n_block, n_block)
        index = (block * line + lax.rem(row // tall, line)) * n_xh + row // (n_block * line * tall)
        member = one(slot == index * CAP + lax.rem(row, CAP)).astype(BF16)
        p = dot(member, s_gate[...])
        q = dot(member, s_up[...])
        sigma = jax.nn.sigmoid(p)
        active = p * sigma
        at = pl.ds(pl.multiple_of(i * f_tile, f_tile), f_tile)
        f_gate[at, :] = q * sigma * (1.0 + p * (1.0 - sigma))
        f_up[at, :] = active
        f_part[at, :] = active * q

    pl.semaphore_wait(barrier, NEAR + n_group - 1 + 3)

    def plane_copy(d):
        return remote(grad, plane_recv.at[g], ps_sem.at[d], pr_sem.at[g], peer(d)[1])

    @pl.loop(1, n_group)
    def _(d):
        plane_copy(d).start()


    own.wait()

    @pl.loop(1, n_group)
    def _(d):
        p, dev = peer(d)
        remote(grad, plane_recv.at[p], ps_sem.at[d], pr_sem.at[p], dev).wait_recv()

    @pl.loop(0, n_group)
    def _(a):
        gathered[pl.ds(pl.multiple_of(a * 8, 8), tok), :] = plane_recv[a].astype(F32)

    slot_rows = sum(
        dot(tables[q], gathered[:, pl.ds(q * part, part)].astype(BF16)) for q in range(QUARTERS)
    ).astype(BF16)
    slots[...] = slot_rows.reshape(n_block, tall, part)

    def far_copy(n):
        to = block_at(-offset_of(n))
        return remote(slots.at[to], x_buf.at[xh, n, r], far_s.at[n], far_r.at[n], far(-offset_of(n)))

    turn = 2 * (1 - 2 * lax.rem(g, 2))
    first_leg, second_leg = {5: 2, 6: -2, 7: turn}, {5: 1, 6: -1, 7: turn}

    def leg_copy(n):
        to = block_at(-offset_of(n))
        at = n - NEAR - 1
        return remote(slots.at[to], relay_x.at[at], far_s.at[n], leg_r.at[at], far(-first_leg[n]))

    def relay_copy(n):
        at = n - NEAR - 1
        return remote(relay_x.at[at], x_buf.at[xh, n, r], relay_s.at[at], far_r.at[n], far(-second_leg[n]))

    for n in (1, 2, 7, 5, 6, 3, 4):
        (far_copy if n <= NEAR else leg_copy)(n).start()
    x_buf[xh, 0, r] = slots[zb]

    def along(n, k, to_right):
        at = x_buf.at[xh, n, k]
        if to_right:
            return remote(at, at, right_s.at[n, k], line_r.at[n, k], right)
        return remote(at, at, left_s.at[n, k], line_r.at[n, k], left)

    def across(n, k):
        at = x_buf.at[xh, n, k]
        return remote(at, at, pair_s.at[n, k], pair_r.at[n, k], pair)

    def when(condition, action):
        pl.when(condition)(action)

    def pass_on(n, d, to_right):
        k = r - d if to_right else r + d

        def arrived():
            along(n, k, to_right).wait_recv()
            when(r < line - 1 if to_right else r > 0, lambda: along(n, k, to_right).start())
            across(n, k).start()

        inside = r >= d if to_right else r + d <= line - 1
        when(inside & (n >= 0) & (n < n_block), arrived)

    per = 4
    n_tile = n_block // per

    def compute(half, i):
        tile = per * line * tall
        row0 = pl.multiple_of((half * n_tile + i) * tile, tile)
        at = pl.ds(row0, tile)
        x = x_buf[half, pl.ds(per * i, per)].reshape(tile, part)
        each = dot_nt(x, w_dn[...])
        q_id = lax.rem(iota((tile, LANES), 0), tall) // CAP
        mine = sum(jnp.where(q_id == q, each[:, q * LANES : (q + 1) * LANES], 0.0) for q in range(QUARTERS))
        mine = mine.reshape(per * line, 2, 8, LANES)
        mine = mine[:, 0] + mine[:, 1]
        mine = mine + pltpu.roll(mine, CAP, 1)
        act = jnp.stack([mine, mine], axis=1).reshape(tile, LANES)
        gate = jnp.sum(f_part[at, :] * act, axis=1, keepdims=True)
        gate_hi = gate.astype(BF16).astype(F32)
        gates = jnp.where(q_id == 0, gate_hi, jnp.where(q_id == 1, gate - gate_hi, 0.0)).astype(BF16)
        pre = [(act * f_gate[at, :]).astype(BF16), (act * f_up[at, :]).astype(BF16)]
        zero = jnp.zeros_like(pre[0])
        spread_pre = jnp.concatenate([jnp.where(q_id == q, v, zero) for q in range(QUARTERS) for v in pre], axis=1)
        out = dot_nt(spread_pre, w_cat[...]).astype(BF16)
        y_buf[half, pl.ds(per * i, per), :, :, pl.ds(0, part)] = out.reshape(per, line, tall, part)
        y_buf[half, pl.ds(per * i, per), :, :, pl.ds(part, LANES)] = gates.reshape(per, line, tall, LANES)

    def add_copy(n):
        return remote(y_buf.at[other, n], pair_sum.at[n], add_s.at[n], add_r.at[n], pair)

    def compute_other(i):
        @pl.loop(0, per * line)
        def _(j):
            n, k = per * i + lax.div(j, line), lax.rem(j, line)
            at = x_buf.at[other, n, k]
            remote(at, at, pair_s.at[n, k], pair_r.at[n, k], pair).wait_recv()

        compute(other, i)

        @pl.loop(0, per)
        def _(j):
            add_copy(per * i + per - 1 - j).start()


    @pl.loop(0, n_block + line - 1)
    def _(step):
        @pl.when(step < n_block)
        def _():
            when(step > 0, lambda: far_copy(step).wait_recv())

            @pl.when(step == 3)
            def _():
                for n in (7, 5, 6):
                    leg_copy(n).wait_recv()
                    relay_copy(n).start()

            when(r < line - 1, lambda: along(step, r, True).start())
            when(r > 0, lambda: along(step, r, False).start())
            across(step, r).start()

        for d in range(1, line):
            pass_on(step - d, d, True)
            pass_on(step - d, d, False)

    for copy in w_copies:
        copy.wait()

    @pl.loop(0, n_tile)
    def _(j):
        compute_other(n_tile - 1 - j)
        compute(xh, n_tile - 1 - j)

    def sum_copy(n, k, to_right):
        src = y_buf.at[xh, n, k]
        if to_right:
            return remote(src, from_left.at[n, k], up_s.at[n, k], up_r.at[n, k], right)
        return remote(src, from_right.at[n, k], down_s.at[n, k], down_r.at[n, k], left)

    def gather_sum(n, k, sides):
        total[...] = y_buf[xh, n, k].astype(F32) + pair_sum[n, k].astype(F32)
        for to_right in sides:

            def add():
                sum_copy(n, k, to_right).wait_recv()
                total[...] += (from_left if to_right else from_right)[n, k].astype(F32)

            when(r > 0 if to_right else r < line - 1, add)

    def send_sum(step, d, to_right):
        p = step - r if to_right else step - (line - 1 - r)
        n = n_block - 1 - p
        k = r + d if to_right else r - d

        def go():
            gather_sum(n, k, (to_right,))
            y_buf[xh, n, k] = total[...].astype(BF16)
            sum_copy(n, k, to_right).start()

        inside = r + d <= line - 1 if to_right else r >= d
        when(inside & (p >= 0) & (p < n_block), go)

    def home_leg(n):
        at = n - NEAR - 1
        return remote(closing.at[n], relay_h.at[at], home_s.at[n], home_leg_r.at[at], far(first_leg[n]))

    def home_relay(n):
        at, origin = n - NEAR - 1, block_at(-first_leg[n])
        return remote(relay_h.at[at], home.at[origin], home_relay_s.at[at], home_r.at[origin], far(second_leg[n]))

    def home_copy(n):
        return remote(closing.at[n], home.at[zb], home_s.at[n], home_r.at[zb], far(offset_of(n)))

    @pl.loop(0, n_block + line - 1)
    def _(step):
        for c, due in ((7, 7), (6, 8), (5, 9)):

            @pl.when(step == due)
            def _():
                home_leg(c).wait_recv()
                home_relay(c).start()

        when(step < n_block, lambda: add_copy(n_block - 1 - step).wait_recv())
        for d in range(line - 1, 0, -1):
            send_sum(step, d, True)
            send_sum(step, d, False)
        n = n_block - 1 - (step - (line - 1))

        @pl.when(n < n_block)
        def _():
            gather_sum(n, r, (True, False))

            @pl.when(n > 0)
            def _():
                closing[n] = total[...].astype(BF16)
                when(n <= NEAR, lambda: home_copy(n).start())
                for c in first_leg:
                    when(n == c, lambda: home_leg(c).start())

            @pl.when(n == 0)
            def _():
                home[zb] = total[...].astype(BF16)

    @pl.loop(1, n_block)
    def _(n):
        e = block_at(-offset_of(n))
        remote(closing.at[n], home.at[e], home_s.at[n], home_r.at[e], far(offset_of(n))).wait_recv()

    sums = home[...].reshape(n_block * tall, wide).astype(F32)
    weighted = sums[:, :part] * slot_weight
    w_hi = weighted.astype(BF16)
    w_low = (weighted - w_hi.astype(F32)).astype(BF16)
    for q in range(QUARTERS):
        gathered[:, pl.ds(q * part, part)] = dot_tn(tables[q], w_hi) + dot_tn(tables[q], w_low)
    f_part[pl.ds(0, n_group * 8), :] = dot_tn(table.astype(BF16), (sums[:, part:] * which_k).astype(BF16))

    @pl.loop(0, n_group)
    def _(a):
        at = pl.ds(pl.multiple_of(a * 8, 8), tok)
        plane_send[a, :, pl.ds(0, D)] = gathered[at, :].astype(BF16)
        plane_send[a, :, pl.ds(D, LANES)] = f_part[at, :].astype(BF16)

    def final_copy(d):
        p, dev = peer(d)
        return remote(plane_send.at[p], final_recv.at[g], fs_sem.at[d], fr_sem.at[g], dev)

    own_final = pltpu.make_async_copy(plane_send.at[g], final_recv.at[g], own_sem.at[1])
    own_final.start()

    @pl.loop(1, n_group)
    def _(d):
        final_copy(d).start()

    @pl.loop(1, n_group)
    def _(d):
        plane_copy(d).wait_send()

    @pl.loop(0, n_block)
    def _(n):
        @pl.when(n > 0)
        def _():
            far_copy(n).wait_send()
            home_copy(n).wait_send()

        add_copy(n).wait_send()

        @pl.loop(0, line)
        def _(k):
            across(n, k).wait_send()
            when((r < line - 1) & (k <= r), lambda: along(n, k, True).wait_send())
            when((r > 0) & (k >= r), lambda: along(n, k, False).wait_send())
            when(k > r, lambda: sum_copy(n, k, True).wait_send())
            when(k < r, lambda: sum_copy(n, k, False).wait_send())

    for n in first_leg:
        relay_copy(n).wait_send()
        home_relay(n).wait_send()
    own_final.wait()

    @pl.loop(1, n_group)
    def _(d):
        p, dev = peer(d)
        remote(plane_send.at[p], final_recv.at[p], fs_sem.at[d], fr_sem.at[p], dev).wait_recv()

    result = lax.fori_loop(
        1, n_group, lambda p, v: v + final_recv[p].astype(F32), final_recv[0].astype(F32)
    )
    grad_in[...] = result[:, :D].astype(BF16)
    grad_gate[...] = result[:, D:].astype(BF16)

    @pl.loop(1, n_group)
    def _(d):
        final_copy(d).wait_send()


def local(n_group, n_local, grad_out, routes, router_weights, gate_weight, up_weight, down_weight, saved_gate, saved_up):
    tok, D = grad_out.shape
    topk = routes.shape[1]
    hid = saved_gate.shape[2]
    n_xh = 2
    n_z = n_local // n_xh
    n_block = EXP_GROUP
    line = n_z // n_block
    part = D // QUARTERS
    wide = part + LANES
    tall = QUARTERS * CAP
    rows = n_local * tall
    dims = (n_group, n_z, n_xh, tok, topk, D)
    vmem = pl.BlockSpec(memory_space=pltpu.VMEM)
    hbm = pl.BlockSpec(memory_space=pl.ANY)
    dma = lambda *shape: pltpu.SemaphoreType.DMA(shape)
    scratch = [
        pltpu.VMEM((n_group, tok, D), BF16),
        pltpu.VMEM((n_group * 8, D), F32),
        pltpu.VMEM((part, 2 * QUARTERS * hid), BF16),
        pltpu.VMEM((QUARTERS * hid, part), BF16),
        pltpu.VMEM((rows, hid), F32),
        pltpu.VMEM((rows, hid), F32),
        pltpu.VMEM((rows, hid), F32),
        pltpu.VMEM((n_block, tall, part), BF16),
        pltpu.VMEM((n_xh, n_block, line, tall, part), BF16),
        pltpu.VMEM((n_xh, n_block, line, tall, wide), BF16),
        pltpu.VMEM((n_block, line, tall, wide), BF16),
        pltpu.VMEM((n_block, line, tall, wide), BF16),
        pltpu.VMEM((n_block, line, tall, wide), BF16),
        pltpu.VMEM((tall, wide), F32),
        pltpu.VMEM((n_block, tall, wide), BF16),
        pltpu.VMEM((n_block, tall, wide), BF16),
        pltpu.VMEM((n_group, tok, D + LANES), BF16),
        pltpu.VMEM((n_group, tok, D + LANES), BF16),
    ]
    scratch += [dma(2), dma(QUARTERS, 3)] + [dma(n_group)] * 4 + [dma(n_block)] * 2
    scratch += [dma(n_block, line)] * 5 + [dma(n_block)] * 2 + [dma(n_block, line)] * 4 + [dma(n_block)] * 2
    n_relay = n_block - 1 - NEAR
    scratch += [pltpu.VMEM((n_relay, tall, part), BF16), pltpu.VMEM((n_relay, tall, wide), BF16)]
    scratch += [dma(n_relay)] * 4
    grad_in, gate = pl.pallas_call(
        functools.partial(kernel, dims),
        out_shape=(
            jax.ShapeDtypeStruct((tok, D), BF16),
            jax.ShapeDtypeStruct((tok, LANES), BF16),
        ),
        in_specs=[vmem] * 5 + [hbm] * 3,
        out_specs=(vmem, vmem),
        scratch_shapes=scratch,
        compiler_params=pltpu.CompilerParams(
            collective_id=0, has_side_effects=True, vmem_limit_bytes=56 * 1024 * 1024
        ),
        cost_estimate=pl.CostEstimate(
            flops=6 * rows * D * hid, bytes_accessed=3 * 2 * D * hid, transcendentals=rows * hid
        ),
    )(grad_out, routes.T, router_weights.T, saved_gate[0], saved_up[0], gate_weight[0], up_weight[0], down_weight[0])
    return grad_in, gate[:, :topk]


def solution(mesh):
    rows = P(("group", "local"), None)
    whole = P(("group", "local"), None, None)
    return jax.shard_map(
        functools.partial(local, mesh.shape["group"], mesh.shape["local"]),
        mesh=mesh,
        in_specs=(rows, P(), P(), whole, whole, whole, whole, whole),
        out_specs=(rows, rows),
        check_vma=False,
    )
```

```python
import functools

import jax
import jax.numpy as jnp
from jax import lax
from jax.experimental import pallas as pl
from jax.experimental.pallas import tpu as pltpu
from jax.sharding import PartitionSpec as P

MESH = pl.DeviceIdType.MESH
EXP_GROUP = 8
CAP = 4
QUARTERS = 4
NEAR = 4
LANES = 128
F32 = jnp.float32
BF16 = jnp.bfloat16


def iota(shape, dim):
    return lax.broadcasted_iota(jnp.int32, shape, dim)


def one(mask):
    return jnp.where(mask, 1.0, 0.0)


def dot(a, b):
    return jnp.dot(a, b, preferred_element_type=F32)


def dot_nt(a, b):
    return lax.dot_general(a, b, (((1,), (1,)), ((), ())), preferred_element_type=F32)


def dot_tn(a, b):
    return lax.dot_general(a, b, (((0,), (0,)), ((), ())), preferred_element_type=F32)


def offset_of(n):
    half = lax.div(n + 1, 2)
    return jnp.where(lax.rem(n, 2) == 1, half, -half)


def kernel(dims, grad, routes_t, weights_t, s_gate, s_up, w_gate, w_up, w_down, grad_in, grad_gate, *scratch):
    n_group, n_z, n_xh, tok, topk, D = dims
    n_local = n_z * n_xh
    n_block = EXP_GROUP
    line = n_z // n_block
    part = D // QUARTERS
    wide = part + LANES
    tall = QUARTERS * CAP
    rows = n_local * tall
    (
        plane_recv, gathered, w_cat, w_dn, f_gate, f_up, f_part, slots, x_buf, y_buf, pair_sum,
        from_left, from_right, total, closing, home, plane_send, final_recv,
        own_sem, w_sem, ps_sem, pr_sem, fs_sem, fr_sem, far_s, far_r, right_s, left_s, line_r, pair_s, pair_r,
        add_s, add_r, up_s, up_r, down_s, down_r, home_s, home_r,
        relay_x, relay_h, leg_r, relay_s, home_leg_r, home_relay_s,
        routes_v, weights_v, s_gate_v, s_up_v, small_sem,
    ) = scratch

    small = [
        pltpu.make_async_copy(src, dst, small_sem.at[i])
        for i, (src, dst) in enumerate(
            [(routes_t, routes_v), (weights_t, weights_v), (s_gate, s_gate_v), (s_up, s_up_v)]
        )
    ]
    for copy in small:
        copy.start()
    g = lax.axis_index("group")
    m = lax.axis_index("local")
    z = m // n_xh
    xh = lax.rem(m, n_xh)
    other = 1 - xh
    zb = z // line
    r = lax.rem(z, line)
    right = (g, lax.rem(m + n_xh, n_local))
    left = (g, lax.rem(m + n_local - n_xh, n_local))
    pair = (g, z * n_xh + other)

    def block_at(offset):
        return lax.rem(zb + offset + n_block, n_block)

    def far(offset):
        return (g, (block_at(offset) * line + r) * n_xh + xh)

    def peer(d):
        p = lax.rem(g + d, n_group)
        return p, (p, m)

    def remote(src, dst, send, recv, dev):
        return pltpu.make_async_remote_copy(src, dst, send, recv, device_id=dev, device_id_type=MESH)

    w_copies = []
    for q in range(QUARTERS):
        cols = pl.ds(q * part, part)
        w_copies += [
            pltpu.make_async_copy(w_down.at[:, cols], w_dn.at[pl.ds(q * LANES, LANES), :], w_sem.at[q, 0]),
            pltpu.make_async_copy(w_gate.at[cols, :], w_cat.at[:, pl.ds(2 * q * LANES, LANES)], w_sem.at[q, 1]),
            pltpu.make_async_copy(w_up.at[cols, :], w_cat.at[:, pl.ds((2 * q + 1) * LANES, LANES)], w_sem.at[q, 2]),
        ]
    own = pltpu.make_async_copy(grad, plane_recv.at[g], own_sem.at[0])
    own.start()
    for copy in w_copies:
        copy.start()

    barrier = pltpu.get_barrier_semaphore()

    def greet(dev):
        pl.semaphore_signal(barrier, inc=1, device_id=dev, device_id_type=MESH)

    @pl.loop(1, NEAR + 1)
    def _(n):
        greet(far(offset_of(n)))

    @pl.loop(1, n_group)
    def _(d):
        greet(peer(d)[1])

    for dev in (left, right, pair):
        greet(dev)

    for copy in small:
        copy.wait()

    lane_r, lane_c = iota((LANES, LANES), 0), iota((LANES, LANES), 1)
    stacked = jnp.concatenate([routes_v[:, pl.ds(a * LANES, LANES)] for a in range(n_group)], axis=0)
    weight = jnp.concatenate([weights_v[:, pl.ds(a * LANES, LANES)] for a in range(n_group)], axis=0)
    t_id = lax.rem(lane_c, 8)
    spread = one((lane_r == m * tok + t_id) & (t_id < tok)).astype(BF16)
    source = one(lane_r // 8 == lane_c // 8)

    def fold(v):
        v = v * source
        return sum(v[a * 8 : a * 8 + 8] for a in range(n_group))

    hi = weight.astype(BF16)
    mid = (weight - hi.astype(F32)).astype(BF16)
    low = (weight - hi.astype(F32) - mid.astype(F32)).astype(BF16)
    own_routes = fold(dot(stacked.astype(F32).astype(BF16), spread))
    own_weights = fold(dot(hi, spread) + dot(mid, spread) + dot(low, spread))
    valid = lax.rem(iota((8, LANES), 1), 8) < tok
    own_routes = jnp.where(valid, own_routes, -1.0)
    first = (g * EXP_GROUP).astype(F32)
    hits, hit_w = [], []
    for e in range(EXP_GROUP):
        same = one(own_routes == first + float(e))
        hits.append(jnp.sum(same, axis=0, keepdims=True))
        hit_w.append(jnp.sum(same * own_weights, axis=0, keepdims=True))
    widen = lambda v: jnp.concatenate([jnp.broadcast_to(t, (tall, LANES)) for t in v], axis=0)
    hit = widen(hits)
    order = dot(hit.astype(BF16), one(lane_r < lane_c).astype(BF16))
    table = hit * one(order == lax.rem(lane_r, CAP).astype(F32))
    quarter = lax.rem(lane_r, tall) // CAP
    slot_weight = jnp.sum(table * widen(hit_w), axis=1, keepdims=True)
    padded = jnp.concatenate([own_routes, jnp.full((LANES - topk, LANES), -1.0, F32)], axis=0)
    slot_routes = dot_nt(table.astype(BF16), padded.astype(BF16))
    which_k = one((slot_routes == first + (lane_r // tall).astype(F32)) & (lane_c < topk))
    tables = [(table * one(quarter == q)).astype(BF16) for q in range(QUARTERS)]

    gathered[...] = jnp.zeros_like(gathered)

    f_tile = 8 * tall

    @pl.loop(0, rows // f_tile)
    def _(i):
        row = iota((f_tile, n_local * CAP), 0) + i * f_tile
        slot = iota((f_tile, n_local * CAP), 1)
        n = lax.rem(row // (line * tall), n_block)
        block = lax.rem(zb + offset_of(n) + n_block, n_block)
        index = (block * line + lax.rem(row // tall, line)) * n_xh + row // (n_block * line * tall)
        member = one(slot == index * CAP + lax.rem(row, CAP)).astype(BF16)
        p = dot(member, s_gate_v[...])
        q = dot(member, s_up_v[...])
        sigma = jax.nn.sigmoid(p)
        active = p * sigma
        at = pl.ds(pl.multiple_of(i * f_tile, f_tile), f_tile)
        f_gate[at, :] = q * sigma * (1.0 + p * (1.0 - sigma))
        f_up[at, :] = active
        f_part[at, :] = active * q

    pl.semaphore_wait(barrier, NEAR + n_group - 1 + 3)

    def plane_copy(d):
        return remote(grad, plane_recv.at[g], ps_sem.at[d], pr_sem.at[g], peer(d)[1])

    @pl.loop(1, n_group)
    def _(d):
        plane_copy(d).start()


    own.wait()

    @pl.loop(1, n_group)
    def _(d):
        p, dev = peer(d)
        remote(grad, plane_recv.at[p], ps_sem.at[d], pr_sem.at[p], dev).wait_recv()

    @pl.loop(0, n_group)
    def _(a):
        gathered[pl.ds(pl.multiple_of(a * 8, 8), tok), :] = plane_recv[a].astype(F32)

    slot_rows = sum(
        dot(tables[q], gathered[:, pl.ds(q * part, part)].astype(BF16)) for q in range(QUARTERS)
    ).astype(BF16)
    slots[...] = slot_rows.reshape(n_block, tall, part)

    def far_copy(n):
        to = block_at(-offset_of(n))
        return remote(slots.at[to], x_buf.at[xh, n, r], far_s.at[n], far_r.at[n], far(-offset_of(n)))

    turn = 2 * (1 - 2 * lax.rem(g, 2))
    first_leg, second_leg = {5: 2, 6: -2, 7: turn}, {5: 1, 6: -1, 7: turn}

    def leg_copy(n):
        to = block_at(-offset_of(n))
        at = n - NEAR - 1
        return remote(slots.at[to], relay_x.at[at], far_s.at[n], leg_r.at[at], far(-first_leg[n]))

    def relay_copy(n):
        at = n - NEAR - 1
        return remote(relay_x.at[at], x_buf.at[xh, n, r], relay_s.at[at], far_r.at[n], far(-second_leg[n]))

    for n in (1, 2, 7, 5, 6, 3, 4):
        (far_copy if n <= NEAR else leg_copy)(n).start()
    x_buf[xh, 0, r] = slots[zb]

    def along(n, k, to_right):
        at = x_buf.at[xh, n, k]
        if to_right:
            return remote(at, at, right_s.at[n, k], line_r.at[n, k], right)
        return remote(at, at, left_s.at[n, k], line_r.at[n, k], left)

    def across(n, k):
        at = x_buf.at[xh, n, k]
        return remote(at, at, pair_s.at[n, k], pair_r.at[n, k], pair)

    def when(condition, action):
        pl.when(condition)(action)

    def pass_on(n, d, to_right):
        k = r - d if to_right else r + d

        def arrived():
            along(n, k, to_right).wait_recv()
            when(r < line - 1 if to_right else r > 0, lambda: along(n, k, to_right).start())
            across(n, k).start()

        inside = r >= d if to_right else r + d <= line - 1
        when(inside & (n >= 0) & (n < n_block), arrived)

    per = 4
    n_tile = n_block // per

    def compute(half, i):
        tile = per * line * tall
        row0 = pl.multiple_of((half * n_tile + i) * tile, tile)
        at = pl.ds(row0, tile)
        x = x_buf[half, pl.ds(per * i, per)].reshape(tile, part)
        each = dot_nt(x, w_dn[...])
        q_id = lax.rem(iota((tile, LANES), 0), tall) // CAP
        mine = sum(jnp.where(q_id == q, each[:, q * LANES : (q + 1) * LANES], 0.0) for q in range(QUARTERS))
        mine = mine.reshape(per * line, 2, 8, LANES)
        mine = mine[:, 0] + mine[:, 1]
        mine = mine + pltpu.roll(mine, CAP, 1)
        act = jnp.stack([mine, mine], axis=1).reshape(tile, LANES)
        gate = jnp.sum(f_part[at, :] * act, axis=1, keepdims=True)
        gate_hi = gate.astype(BF16).astype(F32)
        gates = jnp.where(q_id == 0, gate_hi, jnp.where(q_id == 1, gate - gate_hi, 0.0)).astype(BF16)
        pre = [(act * f_gate[at, :]).astype(BF16), (act * f_up[at, :]).astype(BF16)]
        zero = jnp.zeros_like(pre[0])
        spread_pre = jnp.concatenate([jnp.where(q_id == q, v, zero) for q in range(QUARTERS) for v in pre], axis=1)
        out = dot_nt(spread_pre, w_cat[...]).astype(BF16)
        y_buf[half, pl.ds(per * i, per), :, :, pl.ds(0, part)] = out.reshape(per, line, tall, part)
        y_buf[half, pl.ds(per * i, per), :, :, pl.ds(part, LANES)] = gates.reshape(per, line, tall, LANES)

    def add_copy(n):
        return remote(y_buf.at[other, n], pair_sum.at[n], add_s.at[n], add_r.at[n], pair)

    def compute_other(i):
        @pl.loop(0, per * line)
        def _(j):
            n, k = per * i + lax.div(j, line), lax.rem(j, line)
            at = x_buf.at[other, n, k]
            remote(at, at, pair_s.at[n, k], pair_r.at[n, k], pair).wait_recv()

        compute(other, i)

        @pl.loop(0, per)
        def _(j):
            add_copy(per * i + per - 1 - j).start()


    @pl.loop(0, n_block + 2 * line - 2)
    def _(step):
        @pl.when(step < n_block)
        def _():
            when(step > 0, lambda: far_copy(step).wait_recv())

            @pl.when(step == 3)
            def _():
                for n in (7, 5, 6):
                    leg_copy(n).wait_recv()
                    relay_copy(n).start()

            when(r < line - 1, lambda: along(step, r, True).start())
            when(r > 0, lambda: along(step, r, False).start())
            across(step, r).start()

        for d in range(1, line):
            pass_on(step - 2 * d, d, True)
            pass_on(step - 2 * d, d, False)

    for copy in w_copies:
        copy.wait()

    @pl.loop(0, n_tile)
    def _(j):
        compute_other(n_tile - 1 - j)
        compute(xh, n_tile - 1 - j)

    def sum_copy(n, k, to_right):
        src = y_buf.at[xh, n, k]
        if to_right:
            return remote(src, from_left.at[n, k], up_s.at[n, k], up_r.at[n, k], right)
        return remote(src, from_right.at[n, k], down_s.at[n, k], down_r.at[n, k], left)

    def gather_sum(n, k, sides):
        total[...] = y_buf[xh, n, k].astype(F32) + pair_sum[n, k].astype(F32)
        for to_right in sides:

            def add():
                sum_copy(n, k, to_right).wait_recv()
                total[...] += (from_left if to_right else from_right)[n, k].astype(F32)

            when(r > 0 if to_right else r < line - 1, add)

    def send_sum(step, d, to_right):
        p = step - r if to_right else step - (line - 1 - r)
        n = n_block - 1 - p
        k = r + d if to_right else r - d

        def go():
            gather_sum(n, k, (to_right,))
            y_buf[xh, n, k] = total[...].astype(BF16)
            sum_copy(n, k, to_right).start()

        inside = r + d <= line - 1 if to_right else r >= d
        when(inside & (p >= 0) & (p < n_block), go)

    def home_leg(n):
        at = n - NEAR - 1
        return remote(closing.at[n], relay_h.at[at], home_s.at[n], home_leg_r.at[at], far(first_leg[n]))

    def home_relay(n):
        at, origin = n - NEAR - 1, block_at(-first_leg[n])
        return remote(relay_h.at[at], home.at[origin], home_relay_s.at[at], home_r.at[origin], far(second_leg[n]))

    def home_copy(n):
        return remote(closing.at[n], home.at[zb], home_s.at[n], home_r.at[zb], far(offset_of(n)))

    @pl.loop(0, n_block + line - 1)
    def _(step):
        for c, due in ((7, 7), (6, 8), (5, 9)):

            @pl.when(step == due)
            def _():
                home_leg(c).wait_recv()
                home_relay(c).start()

        when(step < n_block, lambda: add_copy(n_block - 1 - step).wait_recv())
        for d in range(line - 1, 0, -1):
            send_sum(step, d, True)
            send_sum(step, d, False)
        n = n_block - 1 - (step - (line - 1))

        @pl.when(n < n_block)
        def _():
            gather_sum(n, r, (True, False))

            @pl.when(n > 0)
            def _():
                closing[n] = total[...].astype(BF16)
                when(n <= NEAR, lambda: home_copy(n).start())
                for c in first_leg:
                    when(n == c, lambda: home_leg(c).start())

            @pl.when(n == 0)
            def _():
                home[zb] = total[...].astype(BF16)

    @pl.loop(1, n_block)
    def _(n):
        e = block_at(-offset_of(n))
        remote(closing.at[n], home.at[e], home_s.at[n], home_r.at[e], far(offset_of(n))).wait_recv()

    sums = home[...].reshape(n_block * tall, wide).astype(F32)
    weighted = sums[:, :part] * slot_weight
    w_hi = weighted.astype(BF16)
    w_low = (weighted - w_hi.astype(F32)).astype(BF16)
    for q in range(QUARTERS):
        gathered[:, pl.ds(q * part, part)] = dot_tn(tables[q], w_hi) + dot_tn(tables[q], w_low)
    f_part[pl.ds(0, n_group * 8), :] = dot_tn(table.astype(BF16), (sums[:, part:] * which_k).astype(BF16))

    @pl.loop(0, n_group)
    def _(a):
        at = pl.ds(pl.multiple_of(a * 8, 8), tok)
        plane_send[a, :, pl.ds(0, D)] = gathered[at, :].astype(BF16)
        plane_send[a, :, pl.ds(D, LANES)] = f_part[at, :].astype(BF16)

    def final_copy(d):
        p, dev = peer(d)
        return remote(plane_send.at[p], final_recv.at[g], fs_sem.at[d], fr_sem.at[g], dev)

    own_final = pltpu.make_async_copy(plane_send.at[g], final_recv.at[g], own_sem.at[1])
    own_final.start()

    @pl.loop(1, n_group)
    def _(d):
        final_copy(d).start()

    @pl.loop(1, n_group)
    def _(d):
        plane_copy(d).wait_send()

    @pl.loop(0, n_block)
    def _(n):
        @pl.when(n > 0)
        def _():
            far_copy(n).wait_send()
            home_copy(n).wait_send()

        add_copy(n).wait_send()

        @pl.loop(0, line)
        def _(k):
            across(n, k).wait_send()
            when((r < line - 1) & (k <= r), lambda: along(n, k, True).wait_send())
            when((r > 0) & (k >= r), lambda: along(n, k, False).wait_send())
            when(k > r, lambda: sum_copy(n, k, True).wait_send())
            when(k < r, lambda: sum_copy(n, k, False).wait_send())

    for n in first_leg:
        relay_copy(n).wait_send()
        home_relay(n).wait_send()
    own_final.wait()

    @pl.loop(1, n_group)
    def _(d):
        p, dev = peer(d)
        remote(plane_send.at[p], final_recv.at[p], fs_sem.at[d], fr_sem.at[p], dev).wait_recv()

    result = lax.fori_loop(
        1, n_group, lambda p, v: v + final_recv[p].astype(F32), final_recv[0].astype(F32)
    )
    grad_in[...] = result[:, :D].astype(BF16)
    grad_gate[...] = result[:, D:].astype(BF16)

    @pl.loop(1, n_group)
    def _(d):
        final_copy(d).wait_send()


def local(n_group, n_local, grad_out, routes, router_weights, gate_weight, up_weight, down_weight, saved_gate, saved_up):
    tok, D = grad_out.shape
    topk = routes.shape[1]
    hid = saved_gate.shape[2]
    n_xh = 2
    n_z = n_local // n_xh
    n_block = EXP_GROUP
    line = n_z // n_block
    part = D // QUARTERS
    wide = part + LANES
    tall = QUARTERS * CAP
    rows = n_local * tall
    dims = (n_group, n_z, n_xh, tok, topk, D)
    vmem = pl.BlockSpec(memory_space=pltpu.VMEM)
    hbm = pl.BlockSpec(memory_space=pl.ANY)
    dma = lambda *shape: pltpu.SemaphoreType.DMA(shape)
    scratch = [
        pltpu.VMEM((n_group, tok, D), BF16),
        pltpu.VMEM((n_group * 8, D), F32),
        pltpu.VMEM((part, 2 * QUARTERS * hid), BF16),
        pltpu.VMEM((QUARTERS * hid, part), BF16),
        pltpu.VMEM((rows, hid), F32),
        pltpu.VMEM((rows, hid), F32),
        pltpu.VMEM((rows, hid), F32),
        pltpu.VMEM((n_block, tall, part), BF16),
        pltpu.VMEM((n_xh, n_block, line, tall, part), BF16),
        pltpu.VMEM((n_xh, n_block, line, tall, wide), BF16),
        pltpu.VMEM((n_block, line, tall, wide), BF16),
        pltpu.VMEM((n_block, line, tall, wide), BF16),
        pltpu.VMEM((n_block, line, tall, wide), BF16),
        pltpu.VMEM((tall, wide), F32),
        pltpu.VMEM((n_block, tall, wide), BF16),
        pltpu.VMEM((n_block, tall, wide), BF16),
        pltpu.VMEM((n_group, tok, D + LANES), BF16),
        pltpu.VMEM((n_group, tok, D + LANES), BF16),
    ]
    scratch += [dma(2), dma(QUARTERS, 3)] + [dma(n_group)] * 4 + [dma(n_block)] * 2
    scratch += [dma(n_block, line)] * 5 + [dma(n_block)] * 2 + [dma(n_block, line)] * 4 + [dma(n_block)] * 2
    n_relay = n_block - 1 - NEAR
    scratch += [pltpu.VMEM((n_relay, tall, part), BF16), pltpu.VMEM((n_relay, tall, wide), BF16)]
    scratch += [dma(n_relay)] * 4
    scratch += [pltpu.VMEM((topk, routes.shape[0]), jnp.int32), pltpu.VMEM((topk, routes.shape[0]), F32)]
    scratch += [pltpu.VMEM(saved_gate.shape[1:], BF16)] * 2 + [dma(4)]
    grad_in, gate = pl.pallas_call(
        functools.partial(kernel, dims),
        out_shape=(
            jax.ShapeDtypeStruct((tok, D), BF16),
            jax.ShapeDtypeStruct((tok, LANES), BF16),
        ),
        in_specs=[vmem] + [hbm] * 7,
        out_specs=(vmem, vmem),
        scratch_shapes=scratch,
        compiler_params=pltpu.CompilerParams(
            collective_id=0, has_side_effects=True, vmem_limit_bytes=56 * 1024 * 1024
        ),
        cost_estimate=pl.CostEstimate(
            flops=6 * rows * D * hid, bytes_accessed=3 * 2 * D * hid, transcendentals=rows * hid
        ),
    )(grad_out, routes.T, router_weights.T, saved_gate[0], saved_up[0], gate_weight[0], up_weight[0], down_weight[0])
    return grad_in, gate[:, :topk]


def solution(mesh):
    rows = P(("group", "local"), None)
    whole = P(("group", "local"), None, None)
    return jax.shard_map(
        functools.partial(local, mesh.shape["group"], mesh.shape["local"]),
        mesh=mesh,
        in_specs=(rows, P(), P(), whole, whole, whole, whole, whole),
        out_specs=(rows, rows),
        check_vma=False,
    )
```
